256 devices in a mesh: own: 64 (over z, y, core), rep: 4 (over x).
Axes of the slice: x: 4, y: 4, z: 8, core: 2. Of those that a mesh axis runs over, the one named last changes fastest.
Arguments:
- h_in: bfloat16 [32768, 1024], P('own'), may hold values from -16 to 16
- send_rows: int32 [64, 4, 64, 32], P('own', 'rep'), may hold values from 0 to 511
- counts: int32 [64, 4, 64], P('own', 'rep'), may hold values from 1 to 32, as said below
- seed_rows: int32 [64, 4, 256], P('own', 'rep'), may hold values from 0 to 511
- nbr_slot: int32 [64, 4, 256, 8], P('own', 'rep'), may hold values from 0 to 2047, as said below
- degree: int32 [64, 4, 256], P('own', 'rep'), may hold values from 1 to 8
- g_out: bfloat16 [64, 4, 256, 1024], P('own', 'rep'), may hold values from -6 to 6
- weights: bfloat16 [2048, 1024], replicated, may hold values from -0.125 to 0.125
- master: float32 [2048, 1024], P(('own', 'rep')), may hold values from -0.125 to 0.125
- moment: float32 [2048, 1024], P(('own', 'rep')), may hold values from -0.002 to 0.002
- second: float32 [2048, 1024], P(('own', 'rep')), may hold values from 1e-09 to 1e-07
Outputs:
- h_out: bfloat16 [64, 4, 256, 1024], P('own', 'rep')
- grad_in: float32 [32768, 1024], P('own')
- weights_new: bfloat16 [2048, 1024], replicated
- master_new: float32 [2048, 1024], P(('own', 'rep'))
- moment_new: float32 [2048, 1024], P(('own', 'rep'))
- second_new: float32 [2048, 1024], P(('own', 'rep'))
The draws below stay inside these ranges and needn't reach their ends.
Inputs may be any that keep to these rules, and one draw needn't show every extreme that they name: counts[o, r, p] is the used slots of the block from owner o to device (p, r); for each r one destination p gets 32 from every owner. nbr_slot[p, r, s, f] = o * 32 + j names slot j of the block from owner o to device (p, r), with j < counts[o, r, p].
All inputs are finite; a program needn't handle non-finite values.
Results may differ from the reference program's by a relative error of at most 0.004.
Values may be sent and summed in bfloat16 or wider, within the bound.
No kernel may reach another device: no remote copies, remote signals or barrier semaphores. Data moves between devices by JAX's collectives and lax.ppermute only.
A program may use at most 128 MiB of HBM per device.

```python
import math
import jax
import jax.numpy as jnp
from jax import lax

H = 1024
V_DEV = 512
S_DEV = 256
FAN = 8
B = 32
ADAM_STEP = 10
VERTICES = 32768
N_OWN = 64
N_REP = 4


def route_counts(key):
    first_key, other_key = jax.random.split(key)
    base = jax.random.randint(first_key, (N_OWN, N_REP, N_OWN), 1, B + 1)
    hottest = jax.random.randint(other_key, (N_REP,), 0, N_OWN)
    full = jnp.arange(N_OWN)[None, None, :] == hottest[None, :, None]
    return jnp.where(full, B, base).astype(jnp.int32)


def draw_counts(key, part):
    return route_counts(key)


def draw_nbr_slot(key, part):
    limits = route_counts(key)
    key = jax.random.fold_in(key, 7)
    first_key, other_key = jax.random.split(key)
    shape = (N_OWN, N_REP, S_DEV, FAN)
    source = jax.random.randint(first_key, shape, 0, N_OWN)
    pick = jax.random.randint(other_key, shape, 0, 1048576)
    target = jnp.arange(N_OWN)[:, None, None, None]
    replica = jnp.arange(N_REP)[None, :, None, None]
    bound = limits[source, replica, target]
    return (source * B + pick % bound).astype(jnp.int32)


def draw_degree(key, part):
    key = jax.random.fold_in(key, 11)
    drawn = jax.random.randint(key, (N_OWN, N_REP, S_DEV), 1, FAN + 1)
    return drawn.at[:, :, 0].set(FAN).astype(jnp.int32)


def touch_ends(values, own_key, least, top_value):
    longest = values.shape.index(max(values.shape))
    spots = []
    for shift in (0, 1):
        where = [jax.random.randint(jax.random.fold_in(own_key, axis), (), 0, length) for axis, length in enumerate(values.shape)]
        where[longest] = (where[longest] + shift) % values.shape[longest]
        spots.append(tuple(where))
    return values.at[spots[0]].set(least).at[spots[1]].set(top_value)


def strengthened(array, rng, source, target, blocks, factor):
    def block_of(axis_at):
        return (jnp.arange(array.shape[axis_at]) // (array.shape[axis_at] // blocks)).reshape((-1,) + (1,) * (array.ndim - 1 - axis_at))

    near = jax.random.permutation(rng, blocks)[block_of(target)]
    far = (block_of(target) + blocks // 2) % blocks
    return jnp.where((block_of(source) == near) | (block_of(source) == far), factor * array, array)


def level_of(stream_key, extent, cuts, low, top_value):
    def one(dim, shards_of):
        draws = jax.random.uniform(jax.random.fold_in(jax.random.fold_in(stream_key, 6), dim), (shards_of,), jnp.float32, low / len(cuts), top_value / len(cuts))
        return jnp.repeat(jnp.exp(draws), extent[dim] // shards_of).reshape((-1,) + (1,) * (len(extent) - dim - 1))

    factor_of = one(*cuts[0])
    for cut in cuts[1:]:
        factor_of = factor_of * one(*cut)
    return factor_of


def centred(key, shape, deviation, reach, shards=(), kind=jnp.bfloat16):
    entries = jax.random.normal(key, shape, jnp.float32) * deviation
    if len(shards) > 0:
        entries = level_of(key, shape, shards, -0.22, 0.18) * entries
    return jnp.clip(entries, min=-reach, max=reach).astype(kind)


def heavy_noise(key, shape, scale, most, cuts, heavy, kind=jnp.bfloat16):
    entries = scale * jax.random.normal(key, shape, jnp.float32)
    if cuts:
        entries = entries * level_of(key, shape, cuts, -0.22, 0.18)
    return jnp.clip(strengthened(entries, jax.random.fold_in(key, 3), *heavy), -most, most).astype(kind)


def setup_inputs(seed: int = 0) -> dict:
    arg_keys = jax.random.split(jax.random.key(seed), 12)
    return {
        "h_in": heavy_noise(arg_keys[0], (VERTICES, H), 1.0, 16.0, ((0, 64),), (0, 1, 64, 4.0)),
        "send_rows": touch_ends(jax.random.randint(arg_keys[1], (N_OWN, N_REP, N_OWN, B), 0, V_DEV), jax.random.fold_in(arg_keys[1], 1), 0, V_DEV - 1).astype(jnp.int32),
        "counts": draw_counts(jax.random.fold_in(arg_keys[11], 71), 0),
        "seed_rows": touch_ends(jax.random.randint(arg_keys[3], (N_OWN, N_REP, S_DEV), 0, V_DEV), jax.random.fold_in(arg_keys[3], 1), 0, V_DEV - 1).astype(jnp.int32),
        "nbr_slot": draw_nbr_slot(jax.random.fold_in(arg_keys[11], 71), 0),
        "degree": draw_degree(jax.random.fold_in(arg_keys[11], 71), 0),
        "g_out": centred(arg_keys[6], (N_OWN, N_REP, S_DEV, H), 1.0, 6.0, ((0, 64), (1, 4))),
        "weights": centred(arg_keys[7], (2 * H, H), (2 * H) ** -0.5, 0.125),
        "master": centred(arg_keys[8], (2 * H, H), (2 * H) ** -0.5, 0.125, ((0, 256),), jnp.float32),
        "moment": centred(arg_keys[9], (2 * H, H), 0.0003, 0.002, ((0, 256),), jnp.float32),
        "second": jnp.clip(jnp.exp(math.log(1.0000000116860974e-07) - 4.6051702 * jax.random.uniform(arg_keys[10], (2 * H, H), jnp.float32) ** level_of(arg_keys[10], (2 * H, H), ((0, 256),), -0.2, 0.2)), 9.999999717180685e-10, 1.0000000116860974e-07),
    }


beta_first = 0.9
beta_second = 0.999
learning = 0.001
epsilon = 1e-08

def tally_slots(slots, degree, width):
    positions = jnp.arange(width, dtype=jnp.int32)
    total = jnp.zeros((slots.shape[0], width), jnp.float32)
    for column in range(slots.shape[1]):
        matches = (slots[:, column][:, None] == positions[None, :]) & (column < degree)[:, None]
        total = total + matches.astype(jnp.float32)
    return total.astype(jnp.bfloat16)

def device_pass(received, self_rows, slots, degree, cotangent, weights):
    tallies = tally_slots(slots, degree, received.shape[0])
    divisor = degree.astype(jnp.float32)[:, None]
    gathered = (jnp.dot(tallies, received, preferred_element_type=jnp.float32) / divisor).astype(jnp.bfloat16)
    joined = jnp.concatenate([self_rows, gathered], axis=1)
    before = jnp.dot(joined, weights, preferred_element_type=jnp.float32)
    logistic = jax.nn.sigmoid(before)
    h_out = (before * logistic).astype(jnp.bfloat16)
    d_before = (cotangent.astype(jnp.float32) * logistic * (1.0 + before * (1.0 - logistic))).astype(jnp.bfloat16)
    backward = lax.dot_general(d_before, weights, (((1,), (1,)), ((), ())), preferred_element_type=jnp.float32)
    hidden = weights.shape[1]
    d_self = backward[:, :hidden]
    d_scaled = (backward[:, hidden:] / divisor).astype(jnp.bfloat16)
    d_received = lax.dot_general(tallies, d_scaled, (((0,), (0,)), ((), ())), preferred_element_type=jnp.float32).astype(jnp.bfloat16)
    return (h_out, joined, d_before, d_self, d_received)

def adam_update(grad_sum, master, moment, second, seed_total):
    grad = grad_sum / seed_total
    moment_new = beta_first * moment + (1.0 - beta_first) * grad
    second_new = beta_second * second + (1.0 - beta_second) * grad * grad
    corrected_m = moment_new / (1.0 - beta_first ** ADAM_STEP)
    corrected_v = second_new / (1.0 - beta_second ** ADAM_STEP)
    master_new = master - learning * corrected_m / (jnp.sqrt(corrected_v) + epsilon)
    return (master_new, moment_new, second_new)

def reference(h_in, send_rows, counts, seed_rows, nbr_slot, degree, g_out, weights, master, moment, second):
    features = h_in.reshape(N_OWN, V_DEV, H)
    sources = jnp.arange(N_OWN, dtype=jnp.int32)[:, None]
    positions = jnp.arange(B, dtype=jnp.int32)[None, :]

    def visit(carry, device):
        grad_rows, grad_sum = carry
        target = device // N_REP
        replica = device % N_REP
        send_ids = send_rows[:, replica, target]
        filled = positions < counts[:, replica, target][:, None]
        picked = features[sources, send_ids]
        received = jnp.where(filled[:, :, None], picked, jnp.zeros((), jnp.bfloat16)).astype(jnp.bfloat16)
        seed_ids = seed_rows[target, replica]
        self_rows = features[target, seed_ids]
        h_out, joined, d_before, d_self, d_received = device_pass(received.reshape(N_OWN * B, H), self_rows, nbr_slot[target, replica], degree[target, replica], g_out[target, replica], weights)
        kept_grads = jnp.where(filled[:, :, None], d_received.reshape(N_OWN, B, H).astype(jnp.float32), jnp.float32(0.0))
        grad_rows = grad_rows.at[sources, send_ids].add(kept_grads)
        grad_rows = grad_rows.at[target, seed_ids].add(d_self)
        grad_sum = grad_sum + lax.dot_general(joined, d_before, (((0,), (0,)), ((), ())), preferred_element_type=jnp.float32)
        return ((grad_rows, grad_sum), h_out)
    start_carry = (jnp.zeros((N_OWN, V_DEV, H), jnp.float32), jnp.zeros((2 * H, H), jnp.float32))
    (grad_rows, grad_sum), h_all = lax.scan(visit, start_carry, jnp.arange(N_OWN * N_REP, dtype=jnp.int32))
    master_new, moment_new, second_new = adam_update(grad_sum, master, moment, second, float(N_OWN * N_REP * S_DEV))
    return (h_all.reshape(N_OWN, N_REP, S_DEV, H), grad_rows.reshape(N_OWN * V_DEV, H), master_new.astype(jnp.bfloat16), master_new, moment_new, second_new)
```

```python
import jax
import jax.numpy as jnp
import numpy as np
from jax import lax
from jax.sharding import Mesh
from jax.sharding import PartitionSpec as P

ADAM_STEP = 10

beta_first = 0.9
beta_second = 0.999
learning = 0.001
epsilon = 1e-08

OWN = ("z", "y", "c")
ALL = ("z", "y", "c", "x")
bf16 = jnp.bfloat16
f32 = jnp.float32


def dot(a, b, dims=((1,), (0,))):
    return lax.dot_general(a, b, (dims, ((), ())), preferred_element_type=f32)


def exchange(v, axes):
    return lax.all_to_all(v, axes, split_axis=0, concat_axis=0, tiled=True)


def tally_slots(slots, degree, width):
    positions = jnp.arange(width, dtype=jnp.int32)
    total = jnp.zeros((slots.shape[0], width), f32)
    for column in range(slots.shape[1]):
        matches = (slots[:, column][:, None] == positions[None, :]) & (column < degree)[:, None]
        total = total + matches.astype(f32)
    return total.astype(bf16)


def adam_update(grad_sum, master, moment, second, seed_total):
    grad = grad_sum / seed_total
    moment_new = beta_first * moment + (1.0 - beta_first) * grad
    second_new = beta_second * second + (1.0 - beta_second) * grad * grad
    corrected_m = moment_new / (1.0 - beta_first**ADAM_STEP)
    corrected_v = second_new / (1.0 - beta_second**ADAM_STEP)
    master_new = master - learning * corrected_m / (jnp.sqrt(corrected_v) + epsilon)
    return (master_new, moment_new, second_new)


def per_device(
    h_in, send_rows, counts, seed_rows, nbr_slot, degree, g_out, weights, master, moment, second
):
    nz, ny, nc, nx = (lax.axis_size(a) for a in ALL)
    peers, block = send_rows.shape[2:]
    vertices, hidden = h_in.shape
    slots = peers * block
    send_ids = send_rows.reshape(peers, block)
    filled = jnp.arange(block, dtype=jnp.int32)[None, :] < counts.reshape(peers)[:, None]
    picks = jnp.where(filled, send_ids, -1).reshape(slots)
    select = (picks[:, None] == jnp.arange(vertices, dtype=jnp.int32)[None, :]).astype(bf16)
    outgoing = dot(select, h_in).astype(bf16)
    received = exchange(outgoing.reshape(peers, block, hidden), OWN).reshape(slots, hidden)

    seed_ids = seed_rows.reshape(-1)
    seeds = seed_ids.shape[0]
    seed_select = (seed_ids[:, None] == jnp.arange(vertices, dtype=jnp.int32)[None, :]).astype(bf16)
    self_rows = dot(seed_select, h_in).astype(bf16)
    self_before = dot(self_rows, weights[:hidden])

    degree = degree.reshape(seeds)
    tallies = tally_slots(nbr_slot.reshape(seeds, -1), degree, slots)
    divisor = degree.astype(f32)[:, None]
    gathered = (dot(tallies, received) / divisor).astype(bf16)
    before = self_before + dot(gathered, weights[hidden:])
    logistic = jax.nn.sigmoid(before)
    h_out = (before * logistic).astype(bf16)
    cotangent = g_out.reshape(seeds, hidden).astype(f32)
    d_before = (cotangent * logistic * (1.0 + before * (1.0 - logistic))).astype(bf16)
    d_scaled = (dot(d_before, weights[hidden:], ((1,), (1,))) / divisor).astype(bf16)
    d_received = dot(tallies, d_scaled, ((0,), (0,))).astype(bf16)
    returned = exchange(d_received.reshape(peers, block, hidden), OWN).reshape(slots, hidden)

    joined = jnp.concatenate([self_rows, gathered], axis=1)
    grad = dot(joined, d_before, ((0,), (0,)))
    shard = grad.shape[0] // (nz * ny * nc * nx)
    grad = grad.reshape(nz * ny, nc, nx * shard, hidden)
    core = lax.axis_index("c")
    mine = lax.dynamic_index_in_dim(grad, core, 1, keepdims=False)
    other = lax.dynamic_index_in_dim(grad, 1 - core, 1, keepdims=False).astype(bf16)
    mine = mine + lax.ppermute(other, "c", [(0, 1), (1, 0)]).astype(f32)
    mine = mine.astype(bf16).reshape(nz * ny, nx, shard, hidden).transpose(1, 0, 2, 3)
    mine = exchange(mine, "x").astype(f32).sum(0).astype(bf16)
    grad_sum = exchange(mine, ("z", "y")).astype(f32).sum(0)
    seed_total = float(seeds * nz * ny * nc * nx)
    master_new, moment_new, second_new = adam_update(grad_sum, master, moment, second, seed_total)
    part = master_new.astype(bf16)
    part = exchange(jnp.broadcast_to(part[None], (nz * ny, shard, hidden)), ("z", "y"))
    part = exchange(jnp.broadcast_to(part[None], (nx,) + part.shape), "x")
    far = lax.ppermute(part, "c", [(0, 1), (1, 0)])
    pair = jnp.where(core == 0, jnp.stack([part, far]), jnp.stack([far, part]))
    weights_new = pair.transpose(2, 0, 1, 3, 4).reshape(weights.shape)

    d_self = dot(d_before, weights[:hidden], ((1,), (1,)))
    d_high = lax.reduce_precision(d_self, 8, 7)
    d_low = (d_self - d_high).astype(bf16)
    d_high = d_high.astype(bf16)
    owner = dot(select, returned, ((0,), (0,)))
    owner = owner + dot(seed_select, d_high, ((0,), (0,))) + dot(seed_select, d_low, ((0,), (0,)))
    parts = exchange(owner.astype(bf16).reshape(nx, vertices // nx, hidden), "x")
    total = parts.astype(f32).sum(0).astype(bf16)
    grad_in = exchange(jnp.broadcast_to(total[None], parts.shape), "x")
    grad_in = grad_in.reshape(vertices, hidden).astype(f32)
    return (h_out.reshape(g_out.shape), grad_in, weights_new, master_new, moment_new, second_new)


def solution(mesh):
    nx = mesh.shape["rep"]
    devices = np.asarray(mesh.devices).reshape(8, 4, 2, nx)
    return jax.shard_map(
        per_device,
        mesh=Mesh(devices, ALL),
        in_specs=(
            P(OWN, None),
            P(OWN, "x", None, None),
            P(OWN, "x", None),
            P(OWN, "x", None),
            P(OWN, "x", None, None),
            P(OWN, "x", None),
            P(OWN, "x", None, None),
            P(),
            P(ALL, None),
            P(ALL, None),
            P(ALL, None),
        ),
        out_specs=(
            P(OWN, "x", None, None),
            P(OWN, None),
            P(),
            P(ALL, None),
            P(ALL, None),
            P(ALL, None),
        ),
        check_vma=False,
    )
```

```python
import jax
import jax.numpy as jnp
import numpy as np
from jax import lax
from jax.sharding import Mesh
from jax.sharding import PartitionSpec as P

ADAM_STEP = 10

beta_first = 0.9
beta_second = 0.999
learning = 0.001
epsilon = 1e-08

OWN = ("z", "y", "c")
ALL = ("z", "y", "c", "x")
bf16 = jnp.bfloat16
f32 = jnp.float32
CHUNKS = 2


def dot(a, b, dims=((1,), (0,))):
    return lax.dot_general(a, b, (dims, ((), ())), preferred_element_type=f32)


def exchange(v, axes):
    return lax.all_to_all(v, axes, split_axis=0, concat_axis=0, tiled=True)


def shifted(v, axis, step):
    size = lax.axis_size(axis)
    return lax.ppermute(v, axis, [(i, (i + step) % size) for i in range(size)])


def sum_scatter(v, axis, at):
    size, me = lax.axis_size(axis), lax.axis_index(axis)
    block = lambda i: lax.dynamic_index_in_dim(v, i, at, keepdims=False)
    arrived = [
        shifted(block(lax.rem(me + step, size)).astype(bf16), axis, step)
        for step in range(1, size)
    ]
    total = block(me).astype(f32)
    for term in arrived:
        total = total + term.astype(f32)
    return total


def gather_blocks(v, axis, at):
    size, me = lax.axis_size(axis), lax.axis_index(axis)
    shape = v.shape[:at] + (size,) + v.shape[at:]
    whole = lax.dynamic_update_index_in_dim(jnp.zeros(shape, v.dtype), v, me, at)
    for step in range(1, size):
        source = lax.rem(me + size - step, size)
        whole = lax.dynamic_update_index_in_dim(whole, shifted(v, axis, step), source, at)
    return whole


def tally_slots(slots, degree, width):
    positions = jnp.arange(width, dtype=jnp.int32)
    total = jnp.zeros((slots.shape[0], width), f32)
    for column in range(slots.shape[1]):
        matches = (slots[:, column][:, None] == positions[None, :]) & (column < degree)[:, None]
        total = total + matches.astype(f32)
    return total.astype(bf16)


def adam_update(grad_sum, master, moment, second, seed_total):
    grad = grad_sum / seed_total
    moment_new = beta_first * moment + (1.0 - beta_first) * grad
    second_new = beta_second * second + (1.0 - beta_second) * grad * grad
    corrected_m = moment_new / (1.0 - beta_first**ADAM_STEP)
    corrected_v = second_new / (1.0 - beta_second**ADAM_STEP)
    master_new = master - learning * corrected_m / (jnp.sqrt(corrected_v) + epsilon)
    return (master_new, moment_new, second_new)


def per_device(
    h_in, send_rows, counts, seed_rows, nbr_slot, degree, g_out, weights, master, moment, second
):
    nz, ny, nc, nx = (lax.axis_size(a) for a in ALL)
    peers, block = send_rows.shape[2:]
    vertices, hidden = h_in.shape
    slots = peers * block
    send_ids = send_rows.reshape(peers, block)
    filled = jnp.arange(block, dtype=jnp.int32)[None, :] < counts.reshape(peers)[:, None]
    picks = jnp.where(filled, send_ids, -1).reshape(slots)
    select = (picks[:, None] == jnp.arange(vertices, dtype=jnp.int32)[None, :]).astype(bf16)
    outgoing = dot(select, h_in).astype(bf16)
    received = exchange(outgoing.reshape(peers, block, hidden), OWN).reshape(slots, hidden)

    seed_ids = seed_rows.reshape(-1)
    seeds = seed_ids.shape[0]
    seed_select = (seed_ids[:, None] == jnp.arange(vertices, dtype=jnp.int32)[None, :]).astype(bf16)
    self_rows = dot(seed_select, h_in).astype(bf16)
    self_before = dot(self_rows, weights[:hidden])

    degree = degree.reshape(seeds)
    tallies = tally_slots(nbr_slot.reshape(seeds, -1), degree, slots)
    divisor = degree.astype(f32)[:, None]
    gathered = (dot(tallies, received) / divisor).astype(bf16)
    before = self_before + dot(gathered, weights[hidden:])
    logistic = jax.nn.sigmoid(before)
    h_out = (before * logistic).astype(bf16)
    cotangent = g_out.reshape(seeds, hidden).astype(f32)
    d_before = (cotangent * logistic * (1.0 + before * (1.0 - logistic))).astype(bf16)
    d_scaled = (dot(d_before, weights[hidden:], ((1,), (1,))) / divisor).astype(bf16)
    d_received = dot(tallies, d_scaled, ((0,), (0,))).astype(bf16)
    d_before, gathered, d_received = lax.optimization_barrier((d_before, gathered, d_received))
    d_received = d_received.reshape(peers, block, hidden)
    width = hidden // CHUNKS
    returned = [
        exchange(d_received[:, :, i * width : (i + 1) * width], OWN).reshape(slots, width)
        for i in range(CHUNKS)
    ]

    joined = jnp.concatenate([self_rows, gathered], axis=1)
    grad = dot(joined, d_before, ((0,), (0,)))
    shard = grad.shape[0] // (nz * ny * nc * nx)
    grad = grad.reshape(nz, ny, nc, nx, shard, hidden)
    grad = sum_scatter(grad, "c", 2)
    grad = sum_scatter(grad, "x", 2)
    grad = sum_scatter(grad, "y", 1)
    grad_sum = sum_scatter(grad, "z", 0)
    seed_total = float(seeds * nz * ny * nc * nx)
    master_new, moment_new, second_new = adam_update(grad_sum, master, moment, second, seed_total)
    part = master_new.astype(bf16)
    part = gather_blocks(part, "z", 0)
    part = gather_blocks(part, "y", 1)
    part = gather_blocks(part, "x", 2)
    weights_new = gather_blocks(part, "c", 2).reshape(weights.shape)

    d_self = dot(d_before, weights[:hidden], ((1,), (1,)))
    d_high = lax.reduce_precision(d_self, 8, 7)
    d_low = (d_self - d_high).astype(bf16)
    d_high = d_high.astype(bf16)
    owner_self = dot(seed_select, d_high, ((0,), (0,))) + dot(seed_select, d_low, ((0,), (0,)))
    columns = []
    for i in range(CHUNKS):
        owner = dot(select, returned[i], ((0,), (0,))) + owner_self[:, i * width : (i + 1) * width]
        total = sum_scatter(owner.reshape(nx, vertices // nx, width), "x", 0).astype(bf16)
        columns.append(gather_blocks(total, "x", 0).reshape(vertices, width).astype(f32))
    grad_in = jnp.concatenate(columns, axis=1)
    return (h_out.reshape(g_out.shape), grad_in, weights_new, master_new, moment_new, second_new)


def solution(mesh):
    nx = mesh.shape["rep"]
    devices = np.asarray(mesh.devices).reshape(8, 4, 2, nx)
    return jax.shard_map(
        per_device,
        mesh=Mesh(devices, ALL),
        in_specs=(
            P(OWN, None),
            P(OWN, "x", None, None),
            P(OWN, "x", None),
            P(OWN, "x", None),
            P(OWN, "x", None, None),
            P(OWN, "x", None),
            P(OWN, "x", None, None),
            P(),
            P(ALL, None),
            P(ALL, None),
            P(ALL, None),
        ),
        out_specs=(
            P(OWN, "x", None, None),
            P(OWN, None),
            P(),
            P(ALL, None),
            P(ALL, None),
            P(ALL, None),
        ),
        check_vma=False,
    )
```

```python
import jax
import jax.numpy as jnp
import numpy as np
from jax import lax
from jax.experimental import pallas as pl
from jax.experimental.pallas import tpu as pltpu
from jax.sharding import Mesh
from jax.sharding import PartitionSpec as P

ADAM_STEP = 10

beta_first = 0.9
beta_second = 0.999
learning = 0.001
epsilon = 1e-08

OWN = ("z", "y", "c")
ALL = ("z", "y", "c", "x")
bf16 = jnp.bfloat16
f32 = jnp.float32
CHUNKS = 1
TAIL = 16


def dot(a, b, dims=((1,), (0,))):
    return lax.dot_general(a, b, (dims, ((), ())), preferred_element_type=f32)


def exchange(v, axes):
    return lax.all_to_all(v, axes, split_axis=0, concat_axis=0, tiled=True)


def shifted(v, axis, step):
    size = lax.axis_size(axis)
    return lax.ppermute(v, axis, [(i, (i + step) % size) for i in range(size)])


def sum_scatter(v, axis, at):
    size, me = lax.axis_size(axis), lax.axis_index(axis)
    block = lambda i: lax.dynamic_index_in_dim(v, i, at, keepdims=False)
    arrived = [
        shifted(block(lax.rem(me + step, size)).astype(bf16), axis, step)
        for step in range(1, size)
    ]
    total = block(me).astype(f32)
    for term in arrived:
        total = total + term.astype(f32)
    return total


def gather_blocks(v, axis, at):
    size, me = lax.axis_size(axis), lax.axis_index(axis)
    shape = v.shape[:at] + (size,) + v.shape[at:]
    whole = lax.dynamic_update_index_in_dim(jnp.zeros(shape, v.dtype), v, me, at)
    for step in range(1, size):
        source = lax.rem(me + size - step, size)
        whole = lax.dynamic_update_index_in_dim(whole, shifted(v, axis, step), source, at)
    return whole


def tally_slots(slots, width):
    positions = jnp.arange(width, dtype=jnp.int32)
    total = jnp.zeros((slots.shape[0], width), f32)
    for column in range(slots.shape[1]):
        total = total + (slots[:, column][:, None] == positions[None, :]).astype(f32)
    return total.astype(bf16)


def encode_neighbours(neighbours, layer, hidden):
    seeds, fan = neighbours.shape
    codes = jnp.stack([neighbours >> 8, neighbours & 255]) if layer == 256 else None
    rows = codes.astype(bf16).transpose(0, 2, 1).reshape(2 * fan * seeds // hidden, hidden)
    return jnp.pad(rows, ((0, TAIL - rows.shape[0]), (0, 0)))


def layer_rows_kernel(fan, place_ref, packed_ref, *outs):
    seeds, hidden = packed_ref.shape[1] - TAIL, packed_ref.shape[2]
    peers, _, block, width = outs[0].shape
    codes = packed_ref[0, seeds:, :].astype(f32)
    place = place_ref[0].astype(f32)
    positions = lax.broadcasted_iota(jnp.int32, (peers * block, seeds), 0).astype(f32)
    per_row = hidden // seeds
    total = jnp.zeros((peers * block, seeds), f32)
    for f in range(fan):
        row, lane = f // per_row, (f % per_row) * seeds
        which = codes[row : row + 1, lane : lane + seeds]
        slot = codes[fan // per_row + row : fan // per_row + row + 1, lane : lane + seeds]
        slot = jnp.where(which == place, slot, -1.0)
        total = total + (slot == positions).astype(f32)
    rows = dot(total.astype(bf16), packed_ref[0, :seeds, :]).astype(bf16)
    for i, out in enumerate(outs):
        out[...] = rows[:, i * width : (i + 1) * width].reshape(out.shape)


def layer_rows(packed, place, fan, layer, peers, block):
    layers, rows, hidden = packed.shape
    width = hidden // CHUNKS
    shape = (peers, layers, block, width)
    return pl.pallas_call(
        lambda *refs: layer_rows_kernel(fan, *refs),
        grid_spec=pltpu.PrefetchScalarGridSpec(
            num_scalar_prefetch=1,
            grid=(layers,),
            in_specs=[pl.BlockSpec((1, rows, hidden), lambda i, place: (i, 0, 0))],
            out_specs=[pl.BlockSpec((peers, 1, block, width), lambda i, place: (0, i, 0, 0))] * CHUNKS,
        ),
        out_shape=[jax.ShapeDtypeStruct(shape, bf16)] * CHUNKS,
        cost_estimate=pl.CostEstimate(
            flops=2 * layers * layer * (rows - TAIL) * hidden,
            bytes_accessed=2 * (packed.size + layers * layer * hidden),
            transcendentals=0,
        ),
        compiler_params=pltpu.CompilerParams(vmem_limit_bytes=32 * 1024 * 1024),
    )(place.reshape(1), packed)


def adam_update(grad_sum, master, moment, second, seed_total):
    grad = grad_sum / seed_total
    moment_new = beta_first * moment + (1.0 - beta_first) * grad
    second_new = beta_second * second + (1.0 - beta_second) * grad * grad
    corrected_m = moment_new / (1.0 - beta_first**ADAM_STEP)
    corrected_v = second_new / (1.0 - beta_second**ADAM_STEP)
    master_new = master - learning * corrected_m / (jnp.sqrt(corrected_v) + epsilon)
    return (master_new, moment_new, second_new)


def per_device(
    h_in, send_rows, counts, seed_rows, nbr_slot, degree, g_out, weights, master, moment, second
):
    nz, ny, nc, nx = (lax.axis_size(a) for a in ALL)
    peers, block = send_rows.shape[2:]
    vertices, hidden = h_in.shape
    slots = peers * block
    send_ids = send_rows.reshape(peers, block)
    filled = jnp.arange(block, dtype=jnp.int32)[None, :] < counts.reshape(peers)[:, None]
    picks = jnp.where(filled, send_ids, -1).reshape(slots)
    select = (picks[:, None] == jnp.arange(vertices, dtype=jnp.int32)[None, :]).astype(bf16)
    outgoing = dot(select, h_in).astype(bf16)
    received = exchange(outgoing.reshape(peers, block, hidden), OWN).reshape(slots, hidden)

    seed_ids = seed_rows.reshape(-1)
    seeds = seed_ids.shape[0]
    seed_select = (seed_ids[:, None] == jnp.arange(vertices, dtype=jnp.int32)[None, :]).astype(bf16)
    self_rows = dot(seed_select, h_in).astype(bf16)
    self_before = dot(self_rows, weights[:hidden])

    degree = degree.reshape(seeds)
    fan = nbr_slot.shape[-1]
    used = jnp.arange(fan, dtype=jnp.int32)[None, :] < degree[:, None]
    neighbours = jnp.where(used, nbr_slot.reshape(seeds, fan), -1)
    tallies = lax.optimization_barrier(tally_slots(neighbours, slots))
    layer = slots // nz
    tail = encode_neighbours(neighbours, layer, hidden)
    divisor = degree.astype(f32)[:, None]
    gathered = (dot(tallies, received) / divisor).astype(bf16)
    before = self_before + dot(gathered, weights[hidden:])
    logistic = jax.nn.sigmoid(before)
    h_out = (before * logistic).astype(bf16)
    cotangent = g_out.reshape(seeds, hidden).astype(f32)
    d_before = (cotangent * logistic * (1.0 + before * (1.0 - logistic))).astype(bf16)
    d_scaled = (dot(d_before, weights[hidden:], ((1,), (1,))) / divisor).astype(bf16)
    scaled_all = lax.all_gather(jnp.concatenate([d_scaled, tail]), "z", axis=0)
    d_received = layer_rows(scaled_all, lax.axis_index("z"), fan, layer, ny * nc, block)
    width = hidden // CHUNKS

    joined = jnp.concatenate([self_rows, gathered], axis=1)
    grad = dot(joined, d_before, ((0,), (0,)))
    shard = grad.shape[0] // (nz * ny * nc * nx)
    grad = grad.reshape(nz, ny, nc, nx, shard, hidden)
    grad = sum_scatter(grad, "c", 2)
    grad = sum_scatter(grad, "x", 2)
    grad = sum_scatter(grad, "y", 1)
    grad, *d_received = lax.optimization_barrier((grad, *d_received))
    returned = [exchange(part, ("y", "c")).reshape(slots, -1) for part in d_received]
    grad_sum = sum_scatter(grad, "z", 0)
    seed_total = float(seeds * nz * ny * nc * nx)
    master_new, moment_new, second_new = adam_update(grad_sum, master, moment, second, seed_total)
    part = master_new.astype(bf16)
    part = gather_blocks(part, "z", 0)
    part = gather_blocks(part, "x", 1)
    part, *returned = lax.optimization_barrier((part, *returned))
    part = gather_blocks(part, "y", 1)
    weights_new = gather_blocks(part, "c", 2).reshape(weights.shape)

    d_self = dot(d_before, weights[:hidden], ((1,), (1,)))
    d_high = lax.reduce_precision(d_self, 8, 7)
    d_low = (d_self - d_high).astype(bf16)
    d_high = d_high.astype(bf16)
    back = picks.reshape(nz, ny * nc, block).transpose(1, 0, 2).reshape(slots)
    back_select = (back[:, None] == jnp.arange(vertices, dtype=jnp.int32)[None, :]).astype(bf16)
    owner_self = dot(seed_select, d_high, ((0,), (0,))) + dot(seed_select, d_low, ((0,), (0,)))
    columns = []
    for i in range(CHUNKS):
        owner = dot(back_select, returned[i], ((0,), (0,))) + owner_self[:, i * width : (i + 1) * width]
        parts = exchange(owner.astype(bf16).reshape(nx, vertices // nx, width), "x")
        total = parts.astype(f32).sum(0).astype(bf16)
        total = exchange(jnp.broadcast_to(total[None], parts.shape), "x")
        columns.append(total.reshape(vertices, width).astype(f32))
    grad_in = jnp.concatenate(columns, axis=1)
    return (h_out.reshape(g_out.shape), grad_in, weights_new, master_new, moment_new, second_new)


def solution(mesh):
    nx = mesh.shape["rep"]
    devices = np.asarray(mesh.devices).reshape(8, 4, 2, nx)
    return jax.shard_map(
        per_device,
        mesh=Mesh(devices, ALL),
        in_specs=(
            P(OWN, None),
            P(OWN, "x", None, None),
            P(OWN, "x", None),
            P(OWN, "x", None),
            P(OWN, "x", None, None),
            P(OWN, "x", None),
            P(OWN, "x", None, None),
            P(),
            P(ALL, None),
            P(ALL, None),
            P(ALL, None),
        ),
        out_specs=(
            P(OWN, "x", None, None),
            P(OWN, None),
            P(),
            P(ALL, None),
            P(ALL, None),
            P(ALL, None),
        ),
        check_vma=False,
    )
```

```python
import jax
import jax.numpy as jnp
import numpy as np
from jax import lax
from jax.experimental import pallas as pl
from jax.experimental.pallas import tpu as pltpu
from jax.sharding import Mesh
from jax.sharding import PartitionSpec as P

ADAM_STEP = 10

beta_first = 0.9
beta_second = 0.999
learning = 0.001
epsilon = 1e-08

OWN = ("z", "y", "c")
ALL = ("z", "y", "c", "x")
bf16 = jnp.bfloat16
f32 = jnp.float32
CHUNKS = 1
TAIL = 16


def dot(a, b, dims=((1,), (0,))):
    return lax.dot_general(a, b, (dims, ((), ())), preferred_element_type=f32)


def exchange(v, axes):
    return lax.all_to_all(v, axes, split_axis=0, concat_axis=0, tiled=True)


def shifted(v, axis, step):
    size = lax.axis_size(axis)
    return lax.ppermute(v, axis, [(i, (i + step) % size) for i in range(size)])


def sum_scatter(v, axis, at):
    size, me = lax.axis_size(axis), lax.axis_index(axis)
    block = lambda i: lax.dynamic_index_in_dim(v, i, at, keepdims=False)
    arrived = [
        shifted(block(lax.rem(me + step, size)).astype(bf16), axis, step)
        for step in range(1, size)
    ]
    total = block(me).astype(f32)
    for term in arrived:
        total = total + term.astype(f32)
    return total


def gather_blocks(v, axis, at):
    size, me = lax.axis_size(axis), lax.axis_index(axis)
    shape = v.shape[:at] + (size,) + v.shape[at:]
    whole = lax.dynamic_update_index_in_dim(jnp.zeros(shape, v.dtype), v, me, at)
    for step in range(1, size):
        source = lax.rem(me + size - step, size)
        whole = lax.dynamic_update_index_in_dim(whole, shifted(v, axis, step), source, at)
    return whole


def tally_slots(slots, width):
    positions = jnp.arange(width, dtype=jnp.int32)
    total = jnp.zeros((slots.shape[0], width), f32)
    for column in range(slots.shape[1]):
        total = total + (slots[:, column][:, None] == positions[None, :]).astype(f32)
    return total.astype(bf16)


def encode_neighbours(neighbours, layer, hidden):
    seeds, fan = neighbours.shape
    codes = jnp.stack([neighbours >> 8, neighbours & 255]) if layer == 256 else None
    rows = codes.astype(bf16).transpose(0, 2, 1).reshape(2 * fan * seeds // hidden, hidden)
    return jnp.pad(rows, ((0, TAIL - rows.shape[0]), (0, 0)))


def layer_rows_kernel(fan, place_ref, packed_ref, *outs):
    seeds, hidden = packed_ref.shape[1] - TAIL, packed_ref.shape[2]
    peers, _, block, width = outs[0].shape
    codes = packed_ref[0, seeds:, :].astype(f32)
    place = place_ref[0].astype(f32)
    positions = lax.broadcasted_iota(jnp.int32, (peers * block, seeds), 0).astype(f32)
    per_row = hidden // seeds
    total = jnp.zeros((peers * block, seeds), f32)
    for f in range(fan):
        row, lane = f // per_row, (f % per_row) * seeds
        which = codes[row : row + 1, lane : lane + seeds]
        slot = codes[fan // per_row + row : fan // per_row + row + 1, lane : lane + seeds]
        slot = jnp.where(which == place, slot, -1.0)
        total = total + (slot == positions).astype(f32)
    rows = dot(total.astype(bf16), packed_ref[0, :seeds, :]).astype(bf16)
    for i, out in enumerate(outs):
        out[...] = rows[:, i * width : (i + 1) * width].reshape(out.shape)


def layer_rows(packed, place, fan, layer, peers, block):
    layers, rows, hidden = packed.shape
    width = hidden // CHUNKS
    shape = (peers, layers, block, width)
    return pl.pallas_call(
        lambda *refs: layer_rows_kernel(fan, *refs),
        grid_spec=pltpu.PrefetchScalarGridSpec(
            num_scalar_prefetch=1,
            grid=(layers,),
            in_specs=[pl.BlockSpec((1, rows, hidden), lambda i, place: (i, 0, 0))],
            out_specs=[pl.BlockSpec((peers, 1, block, width), lambda i, place: (0, i, 0, 0))] * CHUNKS,
        ),
        out_shape=[pltpu.HBM(shape, bf16)] * CHUNKS,
        cost_estimate=pl.CostEstimate(
            flops=2 * layers * layer * (rows - TAIL) * hidden,
            bytes_accessed=2 * (packed.size + layers * layer * hidden),
            transcendentals=0,
        ),
        compiler_params=pltpu.CompilerParams(vmem_limit_bytes=32 * 1024 * 1024),
    )(place.reshape(1), packed)


def adam_update(grad_sum, master, moment, second, seed_total):
    grad = grad_sum / seed_total
    moment_new = beta_first * moment + (1.0 - beta_first) * grad
    second_new = beta_second * second + (1.0 - beta_second) * grad * grad
    corrected_m = moment_new / (1.0 - beta_first**ADAM_STEP)
    corrected_v = second_new / (1.0 - beta_second**ADAM_STEP)
    master_new = master - learning * corrected_m / (jnp.sqrt(corrected_v) + epsilon)
    return (master_new, moment_new, second_new)


def per_device(
    h_in, send_rows, counts, seed_rows, nbr_slot, degree, g_out, weights, master, moment, second
):
    nz, ny, nc, nx = (lax.axis_size(a) for a in ALL)
    peers, block = send_rows.shape[2:]
    vertices, hidden = h_in.shape
    slots = peers * block
    send_ids = send_rows.reshape(peers, block)
    filled = jnp.arange(block, dtype=jnp.int32)[None, :] < counts.reshape(peers)[:, None]
    picks = jnp.where(filled, send_ids, -1).reshape(slots)
    select = (picks[:, None] == jnp.arange(vertices, dtype=jnp.int32)[None, :]).astype(bf16)
    outgoing = dot(select, h_in).astype(bf16)
    received = exchange(outgoing.reshape(peers, block, hidden), OWN).reshape(slots, hidden)

    seed_ids = seed_rows.reshape(-1)
    seeds = seed_ids.shape[0]
    seed_select = (seed_ids[:, None] == jnp.arange(vertices, dtype=jnp.int32)[None, :]).astype(bf16)
    self_rows = dot(seed_select, h_in).astype(bf16)
    self_before = dot(self_rows, weights[:hidden])

    degree = degree.reshape(seeds)
    fan = nbr_slot.shape[-1]
    used = jnp.arange(fan, dtype=jnp.int32)[None, :] < degree[:, None]
    neighbours = jnp.where(used, nbr_slot.reshape(seeds, fan), -1)
    tallies = lax.optimization_barrier(tally_slots(neighbours, slots))
    layer = slots // nz
    tail = encode_neighbours(neighbours, layer, hidden)
    divisor = degree.astype(f32)[:, None]
    gathered = (dot(tallies, received) / divisor).astype(bf16)
    before = self_before + dot(gathered, weights[hidden:])
    logistic = jax.nn.sigmoid(before)
    h_out = (before * logistic).astype(bf16)
    cotangent = g_out.reshape(seeds, hidden).astype(f32)
    d_before = (cotangent * logistic * (1.0 + before * (1.0 - logistic))).astype(bf16)
    d_scaled = (dot(d_before, weights[hidden:], ((1,), (1,))) / divisor).astype(bf16)
    scaled_all = lax.all_gather(jnp.concatenate([d_scaled, tail]), "z", axis=0)
    d_received = layer_rows(scaled_all, lax.axis_index("z"), fan, layer, ny * nc, block)
    width = hidden // CHUNKS

    joined = jnp.concatenate([self_rows, gathered], axis=1)
    grad = dot(joined, d_before, ((0,), (0,)))
    shard = grad.shape[0] // (nz * ny * nc * nx)
    grad = grad.reshape(nz, ny, nc, nx, shard, hidden)
    grad = sum_scatter(grad, "c", 2)
    grad = sum_scatter(grad, "x", 2)
    grad = sum_scatter(grad, "y", 1)
    grad, *d_received = lax.optimization_barrier((grad, *d_received))
    returned = [exchange(part, ("y", "c")).reshape(slots, -1) for part in d_received]
    grad_sum = sum_scatter(grad, "z", 0)
    seed_total = float(seeds * nz * ny * nc * nx)
    master_new, moment_new, second_new = adam_update(grad_sum, master, moment, second, seed_total)
    part = master_new.astype(bf16)
    part = gather_blocks(part, "z", 0)
    part = gather_blocks(part, "x", 1)
    d_self = dot(d_before, weights[:hidden], ((1,), (1,)))
    d_high = lax.reduce_precision(d_self, 8, 7)
    d_low = (d_self - d_high).astype(bf16)
    d_high = d_high.astype(bf16)
    back = picks.reshape(nz, ny * nc, block).transpose(1, 0, 2).reshape(slots)
    back_select = (back[:, None] == jnp.arange(vertices, dtype=jnp.int32)[None, :]).astype(bf16)
    owner_self = dot(seed_select, d_high, ((0,), (0,))) + dot(seed_select, d_low, ((0,), (0,)))
    part, owner_self, *returned = lax.optimization_barrier((part, owner_self, *returned))
    owner = [
        dot(back_select, piece, ((0,), (0,))) + owner_self[:, i * width : (i + 1) * width]
        for i, piece in enumerate(returned)
    ]
    totals = [
        sum_scatter(rows.reshape(nx, vertices // nx, width), "x", 0).astype(bf16) for rows in owner
    ]
    columns = [gather_blocks(v, "x", 0).reshape(vertices, width) for v in totals]
    part = lax.all_gather(part.reshape(-1, hidden), "y", axis=0, tiled=True)
    part, *columns = lax.optimization_barrier((part, *columns))
    grad_in = jnp.concatenate(columns, axis=1).astype(f32)
    part = part.reshape(ny, nz, nx, shard, hidden).transpose(1, 0, 2, 3, 4)
    weights_new = gather_blocks(part, "c", 2).reshape(weights.shape)
    return (h_out.reshape(g_out.shape), grad_in, weights_new, master_new, moment_new, second_new)


def solution(mesh):
    nx = mesh.shape["rep"]
    devices = np.asarray(mesh.devices).reshape(8, 4, 2, nx)
    return jax.shard_map(
        per_device,
        mesh=Mesh(devices, ALL),
        in_specs=(
            P(OWN, None),
            P(OWN, "x", None, None),
            P(OWN, "x", None),
            P(OWN, "x", None),
            P(OWN, "x", None, None),
            P(OWN, "x", None),
            P(OWN, "x", None, None),
            P(),
            P(ALL, None),
            P(ALL, None),
            P(ALL, None),
        ),
        out_specs=(
            P(OWN, "x", None, None),
            P(OWN, None),
            P(),
            P(ALL, None),
            P(ALL, None),
            P(ALL, None),
        ),
        check_vma=False,
    )
```

```python
import jax
import jax.numpy as jnp
import numpy as np
from jax import lax
from jax.experimental import pallas as pl
from jax.experimental.pallas import tpu as pltpu
from jax.sharding import Mesh
from jax.sharding import PartitionSpec as P

ADAM_STEP = 10

beta_first = 0.9
beta_second = 0.999
learning = 0.001
epsilon = 1e-08

OWN = ("z", "y", "c")
ALL = ("z", "y", "c", "x")
bf16 = jnp.bfloat16
f32 = jnp.float32
CHUNKS = 1
TAIL = 16


def dot(a, b, dims=((1,), (0,))):
    return lax.dot_general(a, b, (dims, ((), ())), preferred_element_type=f32)


def exchange(v, axes):
    return lax.all_to_all(v, axes, split_axis=0, concat_axis=0, tiled=True)


def shifted(v, axis, step):
    size = lax.axis_size(axis)
    return lax.ppermute(v, axis, [(i, (i + step) % size) for i in range(size)])


def sum_scatter(v, axis, at):
    size, me = lax.axis_size(axis), lax.axis_index(axis)
    block = lambda i: lax.dynamic_index_in_dim(v, i, at, keepdims=False)
    arrived = [
        shifted(block(lax.rem(me + step, size)).astype(bf16), axis, step)
        for step in range(1, size)
    ]
    total = block(me).astype(f32)
    for term in arrived:
        total = total + term.astype(f32)
    return total


def gather_blocks(v, axis, at, kind=bf16):
    size, me = lax.axis_size(axis), lax.axis_index(axis)
    shape = v.shape[:at] + (size,) + v.shape[at:]
    whole = lax.dynamic_update_index_in_dim(jnp.zeros(shape, kind), v.astype(kind), me, at)
    for step in range(1, size):
        source = lax.rem(me + size - step, size)
        block = shifted(v, axis, step).astype(kind)
        whole = lax.dynamic_update_index_in_dim(whole, block, source, at)
    return whole


def tally_slots(slots, width):
    positions = jnp.arange(width, dtype=jnp.int32)
    total = jnp.zeros((slots.shape[0], width), f32)
    for column in range(slots.shape[1]):
        total = total + (slots[:, column][:, None] == positions[None, :]).astype(f32)
    return total.astype(bf16)


def encode_neighbours(neighbours, layer, hidden):
    seeds, fan = neighbours.shape
    codes = jnp.stack([neighbours >> 8, neighbours & 255]) if layer == 256 else None
    rows = codes.astype(bf16).transpose(0, 2, 1).reshape(2 * fan * seeds // hidden, hidden)
    return jnp.pad(rows, ((0, TAIL - rows.shape[0]), (0, 0)))


def layer_rows_kernel(fan, place_ref, packed_ref, *outs):
    seeds, hidden = packed_ref.shape[1] - TAIL, packed_ref.shape[2]
    peers, _, block, width = outs[0].shape
    codes = packed_ref[0, seeds:, :].astype(f32)
    place = place_ref[0].astype(f32)
    positions = lax.broadcasted_iota(jnp.int32, (peers * block, seeds), 0).astype(f32)
    per_row = hidden // seeds
    total = jnp.zeros((peers * block, seeds), f32)
    for f in range(fan):
        row, lane = f // per_row, (f % per_row) * seeds
        which = codes[row : row + 1, lane : lane + seeds]
        slot = codes[fan // per_row + row : fan // per_row + row + 1, lane : lane + seeds]
        slot = jnp.where(which == place, slot, -1.0)
        total = total + (slot == positions).astype(f32)
    rows = dot(total.astype(bf16), packed_ref[0, :seeds, :]).astype(bf16)
    for i, out in enumerate(outs):
        out[...] = rows[:, i * width : (i + 1) * width].reshape(out.shape)


def layer_rows(packed, place, fan, layer, peers, block):
    layers, rows, hidden = packed.shape
    width = hidden // CHUNKS
    shape = (peers, layers, block, width)
    return pl.pallas_call(
        lambda *refs: layer_rows_kernel(fan, *refs),
        grid_spec=pltpu.PrefetchScalarGridSpec(
            num_scalar_prefetch=1,
            grid=(layers,),
            in_specs=[pl.BlockSpec((1, rows, hidden), lambda i, place: (i, 0, 0))],
            out_specs=[pl.BlockSpec((peers, 1, block, width), lambda i, place: (0, i, 0, 0))] * CHUNKS,
        ),
        out_shape=[pltpu.HBM(shape, bf16)] * CHUNKS,
        cost_estimate=pl.CostEstimate(
            flops=2 * layers * layer * (rows - TAIL) * hidden,
            bytes_accessed=2 * (packed.size + layers * layer * hidden),
            transcendentals=0,
        ),
        compiler_params=pltpu.CompilerParams(vmem_limit_bytes=32 * 1024 * 1024),
    )(place.reshape(1), pltpu.with_memory_space_constraint(packed, pltpu.HBM))


def adam_update(grad_sum, master, moment, second, seed_total):
    grad = grad_sum / seed_total
    moment_new = beta_first * moment + (1.0 - beta_first) * grad
    second_new = beta_second * second + (1.0 - beta_second) * grad * grad
    corrected_m = moment_new / (1.0 - beta_first**ADAM_STEP)
    corrected_v = second_new / (1.0 - beta_second**ADAM_STEP)
    master_new = master - learning * corrected_m / (jnp.sqrt(corrected_v) + epsilon)
    return (master_new, moment_new, second_new)


def per_device(
    h_in, send_rows, counts, seed_rows, nbr_slot, degree, g_out, weights, master, moment, second
):
    nz, ny, nc, nx = (lax.axis_size(a) for a in ALL)
    peers, block = send_rows.shape[2:]
    vertices, hidden = h_in.shape
    slots = peers * block
    send_ids = send_rows.reshape(peers, block)
    filled = jnp.arange(block, dtype=jnp.int32)[None, :] < counts.reshape(peers)[:, None]
    picks = jnp.where(filled, send_ids, -1).reshape(slots)
    select = (picks[:, None] == jnp.arange(vertices, dtype=jnp.int32)[None, :]).astype(bf16)
    outgoing = dot(select, h_in).astype(bf16)
    received = exchange(outgoing.reshape(peers, block, hidden), OWN).reshape(slots, hidden)

    seed_ids = seed_rows.reshape(-1)
    seeds = seed_ids.shape[0]
    seed_select = (seed_ids[:, None] == jnp.arange(vertices, dtype=jnp.int32)[None, :]).astype(bf16)
    self_rows = dot(seed_select, h_in).astype(bf16)
    self_before = dot(self_rows, weights[:hidden])

    degree = degree.reshape(seeds)
    fan = nbr_slot.shape[-1]
    used = jnp.arange(fan, dtype=jnp.int32)[None, :] < degree[:, None]
    neighbours = jnp.where(used, nbr_slot.reshape(seeds, fan), -1)
    tallies = lax.optimization_barrier(tally_slots(neighbours, slots))
    layer = slots // nz
    tail = encode_neighbours(neighbours, layer, hidden)
    divisor = degree.astype(f32)[:, None]
    gathered = (dot(tallies, received) / divisor).astype(bf16)
    before = self_before + dot(gathered, weights[hidden:])
    logistic = jax.nn.sigmoid(before)
    h_out = (before * logistic).astype(bf16)
    cotangent = g_out.reshape(seeds, hidden).astype(f32)
    d_before = (cotangent * logistic * (1.0 + before * (1.0 - logistic))).astype(bf16)
    d_scaled = (dot(d_before, weights[hidden:], ((1,), (1,))) / divisor).astype(bf16)
    scaled_all = lax.all_gather(jnp.concatenate([d_scaled, tail]), "z", axis=0)
    d_received = layer_rows(scaled_all, lax.axis_index("z"), fan, layer, ny * nc, block)
    width = hidden // CHUNKS

    joined = jnp.concatenate([self_rows, gathered], axis=1)
    grad = dot(joined, d_before, ((0,), (0,)))
    shard = grad.shape[0] // (nz * ny * nc * nx)
    grad = grad.reshape(nz, ny, nc, nx, shard, hidden)
    grad = sum_scatter(grad, "c", 2)
    grad = sum_scatter(grad, "x", 2)
    grad = sum_scatter(grad, "y", 1)
    d_self = dot(d_before, weights[:hidden], ((1,), (1,)))
    d_high = lax.reduce_precision(d_self, 8, 7)
    d_low = (d_self - d_high).astype(bf16)
    d_high = d_high.astype(bf16)
    rows = jnp.arange(vertices, dtype=jnp.int32)[:, None]
    owner_self = dot((rows == seed_ids[None, :]).astype(bf16), jnp.concatenate([d_high, d_low], axis=1))
    owner_self = owner_self[:, :hidden] + owner_self[:, hidden:]
    back = picks.reshape(nz, ny * nc, block).transpose(1, 0, 2).reshape(1, slots)
    back_select = (rows == back).astype(bf16)
    grad, owner_self, back_select, *d_received = lax.optimization_barrier(
        (grad, owner_self, back_select, *d_received)
    )
    returned = [exchange(part, ("y", "c")).reshape(slots, -1) for part in d_received]
    grad_sum = sum_scatter(grad, "z", 0)
    seed_total = float(seeds * nz * ny * nc * nx)
    master_new, moment_new, second_new = adam_update(grad_sum, master, moment, second, seed_total)
    part = master_new.astype(bf16)
    part = gather_blocks(part, "z", 0)
    part = gather_blocks(part, "x", 1)
    part, *returned = lax.optimization_barrier((part, *returned))
    owner = [
        dot(back_select, piece) + owner_self[:, i * width : (i + 1) * width]
        for i, piece in enumerate(returned)
    ]
    totals = [
        sum_scatter(rows.reshape(nx, vertices // nx, width), "x", 0).astype(bf16) for rows in owner
    ]
    columns = [gather_blocks(v, "x", 0, f32).reshape(vertices, width) for v in totals]
    part = lax.all_gather(part.reshape(-1, hidden), "y", axis=0, tiled=True)
    part, *columns = lax.optimization_barrier((part, *columns))
    grad_in = jnp.concatenate(columns, axis=1)
    part = part.reshape(ny, nz, nx, shard, hidden).transpose(1, 0, 2, 3, 4)
    weights_new = gather_blocks(part, "c", 2).reshape(weights.shape)
    return (h_out.reshape(g_out.shape), grad_in, weights_new, master_new, moment_new, second_new)


def solution(mesh):
    nx = mesh.shape["rep"]
    devices = np.asarray(mesh.devices).reshape(8, 4, 2, nx)
    return jax.shard_map(
        per_device,
        mesh=Mesh(devices, ALL),
        in_specs=(
            P(OWN, None),
            P(OWN, "x", None, None),
            P(OWN, "x", None),
            P(OWN, "x", None),
            P(OWN, "x", None, None),
            P(OWN, "x", None),
            P(OWN, "x", None, None),
            P(),
            P(ALL, None),
            P(ALL, None),
            P(ALL, None),
        ),
        out_specs=(
            P(OWN, "x", None, None),
            P(OWN, None),
            P(),
            P(ALL, None),
            P(ALL, None),
            P(ALL, None),
        ),
        check_vma=False,
    )
```

```python
import jax
import jax.numpy as jnp
import numpy as np
from jax import lax
from jax.experimental import pallas as pl
from jax.experimental.pallas import tpu as pltpu
from jax.sharding import Mesh
from jax.sharding import PartitionSpec as P

ADAM_STEP = 10

beta_first = 0.9
beta_second = 0.999
learning = 0.001
epsilon = 1e-08

OWN = ("z", "y", "c")
ALL = ("z", "y", "c", "x")
bf16 = jnp.bfloat16
f32 = jnp.float32
CHUNKS = 1
TAIL = 16


def dot(a, b, dims=((1,), (0,))):
    return lax.dot_general(a, b, (dims, ((), ())), preferred_element_type=f32)


def exchange(v, axes):
    return lax.all_to_all(v, axes, split_axis=0, concat_axis=0, tiled=True)


def shifted(v, axis, step):
    size = lax.axis_size(axis)
    return lax.ppermute(v, axis, [(i, (i + step) % size) for i in range(size)])


def sum_scatter(v, axis, at):
    size, me = lax.axis_size(axis), lax.axis_index(axis)
    block = lambda i: lax.dynamic_index_in_dim(v, i, at, keepdims=False)
    arrived = [
        shifted(block(lax.rem(me + step, size)).astype(bf16), axis, step)
        for step in range(1, size)
    ]
    total = block(me).astype(f32)
    for term in arrived:
        total = total + term.astype(f32)
    return total


def gather_blocks(v, axis, at, kind=bf16):
    size, me = lax.axis_size(axis), lax.axis_index(axis)
    shape = v.shape[:at] + (size,) + v.shape[at:]
    whole = lax.dynamic_update_index_in_dim(jnp.zeros(shape, kind), v.astype(kind), me, at)
    for step in range(1, size):
        source = lax.rem(me + size - step, size)
        block = shifted(v, axis, step).astype(kind)
        whole = lax.dynamic_update_index_in_dim(whole, block, source, at)
    return whole


def tally_slots(slots, width):
    positions = jnp.arange(width, dtype=jnp.int32)
    total = jnp.zeros((slots.shape[0], width), f32)
    for column in range(slots.shape[1]):
        total = total + (slots[:, column][:, None] == positions[None, :]).astype(f32)
    return total.astype(bf16)


def encode_neighbours(neighbours, layer, hidden):
    seeds, fan = neighbours.shape
    codes = jnp.stack([neighbours >> 8, neighbours & 255]) if layer == 256 else None
    rows = codes.astype(bf16).transpose(0, 2, 1).reshape(2 * fan * seeds // hidden, hidden)
    return jnp.pad(rows, ((0, TAIL - rows.shape[0]), (0, 0)))


def layer_rows_kernel(fan, place_ref, packed_ref, *outs):
    seeds, hidden = packed_ref.shape[1] - TAIL, packed_ref.shape[2]
    peers, _, block, width = outs[0].shape
    place = place_ref[0].astype(f32)
    positions = lax.broadcasted_iota(jnp.int32, (peers * block, seeds), 0).astype(f32)
    per_row = hidden // seeds
    for at in range(packed_ref.shape[0]):
        codes = packed_ref[at, seeds:, :].astype(f32)
        total = jnp.zeros((peers * block, seeds), f32)
        for f in range(fan):
            row, lane = f // per_row, (f % per_row) * seeds
            which = codes[row : row + 1, lane : lane + seeds]
            slot = codes[fan // per_row + row : fan // per_row + row + 1, lane : lane + seeds]
            slot = jnp.where(which == place, slot, -1.0)
            total = total + (slot == positions).astype(f32)
        rows = dot(total.astype(bf16), packed_ref[at, :seeds, :]).astype(bf16)
        for i, out in enumerate(outs):
            piece = rows[:, i * width : (i + 1) * width]
            out[:, at, :, :] = piece.reshape(peers, block, width)


def layer_rows(packed, place, fan, layer, peers, block):
    layers, rows, hidden = packed.shape
    width = hidden // CHUNKS
    shape = (peers, layers, block, width)
    each = 2
    return pl.pallas_call(
        lambda *refs: layer_rows_kernel(fan, *refs),
        grid_spec=pltpu.PrefetchScalarGridSpec(
            num_scalar_prefetch=1,
            grid=(layers // each,),
            in_specs=[pl.BlockSpec((each, rows, hidden), lambda i, place: (i, 0, 0))],
            out_specs=[pl.BlockSpec((peers, each, block, width), lambda i, place: (0, i, 0, 0))]
            * CHUNKS,
        ),
        out_shape=[pltpu.HBM(shape, bf16)] * CHUNKS,
        cost_estimate=pl.CostEstimate(
            flops=2 * layers * layer * (rows - TAIL) * hidden,
            bytes_accessed=2 * (packed.size + layers * layer * hidden),
            transcendentals=0,
        ),
        compiler_params=pltpu.CompilerParams(vmem_limit_bytes=32 * 1024 * 1024),
    )(place.reshape(1), pltpu.with_memory_space_constraint(packed, pltpu.HBM))


def adam_update(grad_sum, master, moment, second, seed_total):
    grad = grad_sum / seed_total
    moment_new = beta_first * moment + (1.0 - beta_first) * grad
    second_new = beta_second * second + (1.0 - beta_second) * grad * grad
    corrected_m = moment_new / (1.0 - beta_first**ADAM_STEP)
    corrected_v = second_new / (1.0 - beta_second**ADAM_STEP)
    master_new = master - learning * corrected_m / (jnp.sqrt(corrected_v) + epsilon)
    return (master_new, moment_new, second_new)


def per_device(
    h_in, send_rows, counts, seed_rows, nbr_slot, degree, g_out, weights, master, moment, second
):
    nz, ny, nc, nx = (lax.axis_size(a) for a in ALL)
    peers, block = send_rows.shape[2:]
    vertices, hidden = h_in.shape
    slots = peers * block
    send_ids = send_rows.reshape(peers, block)
    filled = jnp.arange(block, dtype=jnp.int32)[None, :] < counts.reshape(peers)[:, None]
    picks = jnp.where(filled, send_ids, -1).reshape(slots)
    select = (picks[:, None] == jnp.arange(vertices, dtype=jnp.int32)[None, :]).astype(bf16)
    outgoing = dot(select, h_in).astype(bf16)
    received = exchange(outgoing.reshape(peers, block, hidden), OWN).reshape(slots, hidden)

    seed_ids = seed_rows.reshape(-1)
    seeds = seed_ids.shape[0]
    seed_select = (seed_ids[:, None] == jnp.arange(vertices, dtype=jnp.int32)[None, :]).astype(bf16)
    self_rows = dot(seed_select, h_in).astype(bf16)
    self_before = dot(self_rows, weights[:hidden])

    degree = degree.reshape(seeds)
    fan = nbr_slot.shape[-1]
    used = jnp.arange(fan, dtype=jnp.int32)[None, :] < degree[:, None]
    neighbours = jnp.where(used, nbr_slot.reshape(seeds, fan), -1)
    tallies = lax.optimization_barrier(tally_slots(neighbours, slots))
    layer = slots // nz
    tail = encode_neighbours(neighbours, layer, hidden)
    divisor = degree.astype(f32)[:, None]
    gathered = (dot(tallies, received) / divisor).astype(bf16)
    before = self_before + dot(gathered, weights[hidden:])
    logistic = jax.nn.sigmoid(before)
    h_out = (before * logistic).astype(bf16)
    cotangent = g_out.reshape(seeds, hidden).astype(f32)
    d_before = (cotangent * logistic * (1.0 + before * (1.0 - logistic))).astype(bf16)
    d_scaled = (dot(d_before, weights[hidden:], ((1,), (1,))) / divisor).astype(bf16)
    scaled_all = lax.all_gather(jnp.concatenate([d_scaled, tail]), "z", axis=0)
    d_received = layer_rows(scaled_all, lax.axis_index("z"), fan, layer, ny * nc, block)
    width = hidden // CHUNKS

    joined = jnp.concatenate([self_rows, gathered], axis=1)
    grad = dot(joined, d_before, ((0,), (0,)))
    shard = grad.shape[0] // (nz * ny * nc * nx)
    grad = grad.reshape(nz, ny, nc, nx, shard, hidden)
    grad = sum_scatter(grad, "c", 2)
    grad = sum_scatter(grad, "x", 2)
    grad = sum_scatter(grad, "y", 1)
    d_self = dot(d_before, weights[:hidden], ((1,), (1,)))
    d_high = lax.reduce_precision(d_self, 8, 7)
    d_low = (d_self - d_high).astype(bf16)
    d_high = d_high.astype(bf16)
    rows = jnp.arange(vertices, dtype=jnp.int32)[:, None]
    owner_self = dot((rows == seed_ids[None, :]).astype(bf16), jnp.concatenate([d_high, d_low], axis=1))
    owner_self = owner_self[:, :hidden] + owner_self[:, hidden:]
    back = picks.reshape(nz, ny * nc, block).transpose(1, 0, 2).reshape(1, slots)
    back_select = (rows == back).astype(bf16)
    grad, owner_self, back_select, *d_received = lax.optimization_barrier(
        (grad, owner_self, back_select, *d_received)
    )
    returned = [exchange(part, ("y", "c")).reshape(slots, -1) for part in d_received]
    grad_sum = sum_scatter(grad, "z", 0)
    seed_total = float(seeds * nz * ny * nc * nx)
    master_new, moment_new, second_new = adam_update(grad_sum, master, moment, second, seed_total)
    part = master_new.astype(bf16)
    part = gather_blocks(part, "z", 0)
    part = gather_blocks(part, "x", 1)
    part, *returned = lax.optimization_barrier((part, *returned))
    owner = [
        dot(back_select, piece) + owner_self[:, i * width : (i + 1) * width]
        for i, piece in enumerate(returned)
    ]
    totals = [
        sum_scatter(rows.reshape(nx, vertices // nx, width), "x", 0).astype(bf16) for rows in owner
    ]
    columns = [gather_blocks(v, "x", 0, f32).reshape(vertices, width) for v in totals]
    part = lax.all_gather(part.reshape(-1, hidden), "y", axis=0, tiled=True)
    part, *columns = lax.optimization_barrier((part, *columns))
    grad_in = jnp.concatenate(columns, axis=1)
    part = part.reshape(ny, nz, nx, shard, hidden).transpose(1, 0, 2, 3, 4)
    weights_new = gather_blocks(part, "c", 2).reshape(weights.shape)
    return (h_out.reshape(g_out.shape), grad_in, weights_new, master_new, moment_new, second_new)


def solution(mesh):
    nx = mesh.shape["rep"]
    devices = np.asarray(mesh.devices).reshape(8, 4, 2, nx)
    return jax.shard_map(
        per_device,
        mesh=Mesh(devices, ALL),
        in_specs=(
            P(OWN, None),
            P(OWN, "x", None, None),
            P(OWN, "x", None),
            P(OWN, "x", None),
            P(OWN, "x", None, None),
            P(OWN, "x", None),
            P(OWN, "x", None, None),
            P(),
            P(ALL, None),
            P(ALL, None),
            P(ALL, None),
        ),
        out_specs=(
            P(OWN, "x", None, None),
            P(OWN, None),
            P(),
            P(ALL, None),
            P(ALL, None),
            P(ALL, None),
        ),
        check_vma=False,
    )
```

```python
import jax
import jax.numpy as jnp
import numpy as np
from jax import lax
from jax.experimental import pallas as pl
from jax.experimental.pallas import tpu as pltpu
from jax.sharding import Mesh
from jax.sharding import PartitionSpec as P

ADAM_STEP = 10

beta_first = 0.9
beta_second = 0.999
learning = 0.001
epsilon = 1e-08

OWN = ("z", "y", "c")
ALL = ("z", "y", "c", "x")
bf16 = jnp.bfloat16
f32 = jnp.float32
CHUNKS = 1
TAIL = 16


def dot(a, b, dims=((1,), (0,))):
    return lax.dot_general(a, b, (dims, ((), ())), preferred_element_type=f32)


def exchange(v, axes):
    return lax.all_to_all(v, axes, split_axis=0, concat_axis=0, tiled=True)


def shifted(v, axis, step):
    size = lax.axis_size(axis)
    return lax.ppermute(v, axis, [(i, (i + step) % size) for i in range(size)])


def sum_scatter(v, axis, at):
    size, me = lax.axis_size(axis), lax.axis_index(axis)
    block = lambda i: lax.dynamic_index_in_dim(v, i, at, keepdims=False)
    arrived = [
        shifted(block(lax.rem(me + step, size)).astype(bf16), axis, step)
        for step in range(1, size)
    ]
    total = block(me).astype(f32)
    for term in arrived:
        total = total + term.astype(f32)
    return total


def gather_blocks(v, axis, at, kind=bf16, arrived=None):
    size, me = lax.axis_size(axis), lax.axis_index(axis)
    shape = v.shape[:at] + (size,) + v.shape[at:]
    whole = lax.dynamic_update_index_in_dim(jnp.zeros(shape, kind), v.astype(kind), me, at)
    for step in range(1, size):
        source = lax.rem(me + size - step, size)
        block = shifted(v, axis, step) if arrived is None else arrived[step - 1]
        block = block.astype(kind)
        whole = lax.dynamic_update_index_in_dim(whole, block, source, at)
    return whole


def tally_slots(slots, width):
    positions = jnp.arange(width, dtype=jnp.int32)
    total = jnp.zeros((slots.shape[0], width), f32)
    for column in range(slots.shape[1]):
        total = total + (slots[:, column][:, None] == positions[None, :]).astype(f32)
    return total.astype(bf16)


def encode_neighbours(neighbours, layer, hidden):
    seeds, fan = neighbours.shape
    codes = jnp.stack([neighbours >> 8, neighbours & 255]) if layer == 256 else None
    rows = codes.astype(bf16).transpose(0, 2, 1).reshape(2 * fan * seeds // hidden, hidden)
    return jnp.pad(rows, ((0, TAIL - rows.shape[0]), (0, 0)))


def layer_rows_kernel(fan, place_ref, packed_ref, *outs):
    seeds, hidden = packed_ref.shape[1] - TAIL, packed_ref.shape[2]
    peers, _, block, width = outs[0].shape
    place = place_ref[0].astype(f32)
    positions = lax.broadcasted_iota(jnp.int32, (peers * block, seeds), 0).astype(f32)
    per_row = hidden // seeds
    for at in range(packed_ref.shape[0]):
        codes = packed_ref[at, seeds:, :].astype(f32)
        total = jnp.zeros((peers * block, seeds), f32)
        for f in range(fan):
            row, lane = f // per_row, (f % per_row) * seeds
            which = codes[row : row + 1, lane : lane + seeds]
            slot = codes[fan // per_row + row : fan // per_row + row + 1, lane : lane + seeds]
            slot = jnp.where(which == place, slot, -1.0)
            total = total + (slot == positions).astype(f32)
        rows = dot(total.astype(bf16), packed_ref[at, :seeds, :]).astype(bf16)
        for i, out in enumerate(outs):
            piece = rows[:, i * width : (i + 1) * width]
            out[:, at, :, :] = piece.reshape(peers, block, width)


def layer_rows(packed, place, fan, layer, peers, block):
    layers, rows, hidden = packed.shape
    width = hidden // CHUNKS
    shape = (peers, layers, block, width)
    each = 2
    return pl.pallas_call(
        lambda *refs: layer_rows_kernel(fan, *refs),
        grid_spec=pltpu.PrefetchScalarGridSpec(
            num_scalar_prefetch=1,
            grid=(layers // each,),
            in_specs=[pl.BlockSpec((each, rows, hidden), lambda i, place: (i, 0, 0))],
            out_specs=[pl.BlockSpec((peers, each, block, width), lambda i, place: (0, i, 0, 0))]
            * CHUNKS,
        ),
        out_shape=[pltpu.HBM(shape, bf16)] * CHUNKS,
        cost_estimate=pl.CostEstimate(
            flops=2 * layers * layer * (rows - TAIL) * hidden,
            bytes_accessed=2 * (packed.size + layers * layer * hidden),
            transcendentals=0,
        ),
        compiler_params=pltpu.CompilerParams(vmem_limit_bytes=32 * 1024 * 1024),
    )(place.reshape(1), pltpu.with_memory_space_constraint(packed, pltpu.HBM))


def adam_update(grad_sum, master, moment, second, seed_total):
    grad = grad_sum / seed_total
    moment_new = beta_first * moment + (1.0 - beta_first) * grad
    second_new = beta_second * second + (1.0 - beta_second) * grad * grad
    corrected_m = moment_new / (1.0 - beta_first**ADAM_STEP)
    corrected_v = second_new / (1.0 - beta_second**ADAM_STEP)
    master_new = master - learning * corrected_m / (jnp.sqrt(corrected_v) + epsilon)
    return (master_new, moment_new, second_new)


def per_device(
    h_in, send_rows, counts, seed_rows, nbr_slot, degree, g_out, weights, master, moment, second
):
    nz, ny, nc, nx = (lax.axis_size(a) for a in ALL)
    peers, block = send_rows.shape[2:]
    vertices, hidden = h_in.shape
    slots = peers * block
    send_ids = send_rows.reshape(peers, block)
    filled = jnp.arange(block, dtype=jnp.int32)[None, :] < counts.reshape(peers)[:, None]
    picks = jnp.where(filled, send_ids, -1).reshape(slots)
    select = (picks[:, None] == jnp.arange(vertices, dtype=jnp.int32)[None, :]).astype(bf16)
    outgoing = dot(select, h_in).astype(bf16)
    received = exchange(outgoing.reshape(peers, block, hidden), OWN).reshape(slots, hidden)

    seed_ids = seed_rows.reshape(-1)
    seeds = seed_ids.shape[0]
    seed_select = (seed_ids[:, None] == jnp.arange(vertices, dtype=jnp.int32)[None, :]).astype(bf16)
    self_rows = dot(seed_select, h_in).astype(bf16)
    self_before = dot(self_rows, weights[:hidden])

    degree = degree.reshape(seeds)
    fan = nbr_slot.shape[-1]
    used = jnp.arange(fan, dtype=jnp.int32)[None, :] < degree[:, None]
    neighbours = jnp.where(used, nbr_slot.reshape(seeds, fan), -1)
    tallies = lax.optimization_barrier(tally_slots(neighbours, slots))
    layer = slots // nz
    tail = encode_neighbours(neighbours, layer, hidden)
    divisor = degree.astype(f32)[:, None]
    gathered = (dot(tallies, received) / divisor).astype(bf16)
    before = self_before + dot(gathered, weights[hidden:])
    logistic = jax.nn.sigmoid(before)
    h_out = (before * logistic).astype(bf16)
    cotangent = g_out.reshape(seeds, hidden).astype(f32)
    d_before = (cotangent * logistic * (1.0 + before * (1.0 - logistic))).astype(bf16)
    d_scaled = (dot(d_before, weights[hidden:], ((1,), (1,))) / divisor).astype(bf16)
    scaled_all = lax.all_gather(jnp.concatenate([d_scaled, tail]), "z", axis=0)
    d_received = layer_rows(scaled_all, lax.axis_index("z"), fan, layer, ny * nc, block)
    width = hidden // CHUNKS

    joined = jnp.concatenate([self_rows, gathered], axis=1)
    grad = dot(joined, d_before, ((0,), (0,)))
    shard = grad.shape[0] // (nz * ny * nc * nx)
    grad = grad.reshape(nz, ny, nc, nx, shard, hidden)
    grad = sum_scatter(grad, "c", 2)
    grad = sum_scatter(grad, "x", 2)
    grad = sum_scatter(grad, "y", 1)
    d_self = dot(d_before, weights[:hidden], ((1,), (1,)))
    d_high = lax.reduce_precision(d_self, 8, 7)
    d_low = (d_self - d_high).astype(bf16)
    d_high = d_high.astype(bf16)
    rows = jnp.arange(vertices, dtype=jnp.int32)[:, None]
    owner_self = dot((rows == seed_ids[None, :]).astype(bf16), jnp.concatenate([d_high, d_low], axis=1))
    owner_self = owner_self[:, :hidden] + owner_self[:, hidden:]
    back = picks.reshape(nz, ny * nc, block).transpose(1, 0, 2).reshape(1, slots)
    back_select = (rows == back).astype(bf16)
    grad, owner_self, back_select, *d_received = lax.optimization_barrier(
        (grad, owner_self, back_select, *d_received)
    )
    returned = [exchange(part, ("y", "c")).reshape(slots, -1) for part in d_received]
    grad_sum = sum_scatter(grad, "z", 0)
    seed_total = float(seeds * nz * ny * nc * nx)
    master_new, moment_new, second_new = adam_update(grad_sum, master, moment, second, seed_total)
    part = master_new.astype(bf16)
    part = gather_blocks(part, "z", 0)
    part = gather_blocks(part, "x", 1)
    part, *returned = lax.optimization_barrier((part, *returned))
    owner = [
        dot(back_select, piece) + owner_self[:, i * width : (i + 1) * width]
        for i, piece in enumerate(returned)
    ]
    totals = [
        sum_scatter(rows.reshape(nx, vertices // nx, width), "x", 0).astype(bf16) for rows in owner
    ]
    arrived = [[shifted(v, "x", step) for step in range(1, nx)] for v in totals]
    part = lax.all_gather(part.reshape(-1, hidden), "y", axis=0, tiled=True)
    part, arrived = lax.optimization_barrier((part, arrived))
    columns = [
        gather_blocks(v, "x", 0, f32, blocks).reshape(vertices, width)
        for v, blocks in zip(totals, arrived)
    ]
    grad_in = jnp.concatenate(columns, axis=1)
    part = part.reshape(ny, nz, nx, shard, hidden).transpose(1, 0, 2, 3, 4)
    weights_new = gather_blocks(part, "c", 2).reshape(weights.shape)
    return (h_out.reshape(g_out.shape), grad_in, weights_new, master_new, moment_new, second_new)


def solution(mesh):
    nx = mesh.shape["rep"]
    devices = np.asarray(mesh.devices).reshape(8, 4, 2, nx)
    return jax.shard_map(
        per_device,
        mesh=Mesh(devices, ALL),
        in_specs=(
            P(OWN, None),
            P(OWN, "x", None, None),
            P(OWN, "x", None),
            P(OWN, "x", None),
            P(OWN, "x", None, None),
            P(OWN, "x", None),
            P(OWN, "x", None, None),
            P(),
            P(ALL, None),
            P(ALL, None),
            P(ALL, None),
        ),
        out_specs=(
            P(OWN, "x", None, None),
            P(OWN, None),
            P(),
            P(ALL, None),
            P(ALL, None),
            P(ALL, None),
        ),
        check_vma=False,
    )
```
